32 devices in a mesh: band: 2 (over y), row: 4 (over x, core), col: 4 (over z).
Axes of the slice: x: 2, y: 2, z: 4, core: 2. Of those that a mesh axis runs over, the one named last changes fastest.
Arguments:
- orbitals: bfloat16 [64, 64, 64, 128], P('band', 'row', 'col'), may hold values from -6 to 6
- band_ranking: int32 [2, 32], P('band'), may hold values from 0 to 31, each once within a row
- pool_states: bfloat16 [8, 64, 64, 128], P(None, 'row', 'col'), may hold values from -6 to 6
- state_order: int32 [8], replicated, may hold values from 0 to 7, each once
- gvector_index: int32 [24576], replicated, may hold values from 0 to 524287, as said below
- screened: bfloat16 [2, 24576, 24576], P(None, ('band', 'row'), 'col'), may hold values from -0.00024414062 to 0.00024414062
Outputs:
- sigma: float32 [2, 2, 2, 32], replicated
The draws below stay inside these ranges and needn't reach their ends.
Inputs may be any that keep to these rules, and one draw needn't show every extreme that they name: `band_ranking`: each row holds every number of 0 to 31 once. `state_order`: holds every number of 0 to 7 once. `gvector_index`: 24576 distinct flat indices (kx 64 + ky) * 128 + kz into the transform grid.
All inputs are finite; a program needn't handle non-finite values.
Results may differ from the reference program's by a relative error of at most 0.0059.
Values may be sent and summed in bfloat16 or wider, within the bound.
A program may use at most 192 MiB of HBM per device.

```python
import math
import jax
import jax.numpy as jnp
from jax import lax

NX = 64
NY = 64
NZ = 128
NG = 24576
GB = 16
NQ = 2
POOL = 8
STORED = 32
GROUPS = 2
NB = 32
NP = 64
RB = 3072


def signed_frequency(wave, length):
    return (wave + length // 2) % length - length // 2


def draw_gvector_index(key, part):
    total = NX * NY * NZ
    widest = max(NX, NY, NZ)
    flat = jnp.arange(total, dtype=jnp.int32)
    wave_x = flat // (NY * NZ)
    wave_y = flat // NZ % NY
    wave_z = flat % NZ
    length_x = signed_frequency(wave_x, NX) * (widest // NX)
    length_y = signed_frequency(wave_y, NY) * (widest // NY)
    length_z = signed_frequency(wave_z, NZ) * (widest // NZ)
    squared = length_x * length_x + length_y * length_y + length_z * length_z
    shuffle = jax.random.permutation(key, total).astype(jnp.int32)
    shuffled = jnp.take(squared, shuffle)
    ranked = jnp.argsort(shuffled, stable=True)
    return jnp.take(shuffle, ranked[:NG]).astype(jnp.int32)


def shard_levels(stream_key, extent, split, smallest, largest):
    factor_of, own = 1.0, jax.random.fold_in(stream_key, 6)
    for position, parts in split:
        draws = jnp.exp(jax.random.uniform(jax.random.fold_in(own, position), (parts,), jnp.float32, smallest / len(split), largest / len(split)))
        factor_of = factor_of * jnp.repeat(draws, extent[position] // parts).reshape([-1 if axis == position else 1 for axis in range(len(extent))])
    return factor_of


def normal_values(rng, dims, scale, limit, shards=(), held_as=jnp.bfloat16):
    factor_of = shard_levels(rng, dims, shards, -0.22, 0.18) if shards else 1.0
    drawn = jax.random.normal(rng, dims, jnp.float32) * scale * factor_of
    return jnp.minimum(jnp.maximum(drawn, -limit), limit).astype(held_as)


def setup_inputs(seed: int = 0) -> dict:
    keys = jax.random.split(jax.random.key(seed), 7)
    orbitals = normal_values(keys[0], (STORED * GROUPS, NX, NY, NZ), 1.0, 6.0, ((0, 2), (1, 4), (2, 4)))
    band_ranking = jax.vmap(lambda own: jax.random.permutation(own, STORED))(jax.random.split(keys[1], GROUPS)).reshape((GROUPS, STORED)).astype(jnp.int32)
    pool_states = normal_values(keys[2], (POOL, NX, NY, NZ), 1.0, 6.0, ((1, 4), (2, 4)))
    state_order = jax.random.permutation(keys[3], POOL).astype(jnp.int32)
    gvector_index = draw_gvector_index(jax.random.fold_in(keys[6], 71), 0)
    screened = normal_values(keys[5], (2, NG, NG), (NG * NG) ** -0.5, 0.00024414062, ((1, 8), (2, 4)))
    return dict(orbitals=orbitals, band_ranking=band_ranking, pool_states=pool_states, state_order=state_order, gvector_index=gvector_index, screened=screened)


def pick_window(held, wanted):
    return jnp.take(held, wanted.astype(jnp.int32), axis=0)

def reference(orbitals, band_ranking, pool_states, state_order, gvector_index, screened):
    grouped = orbitals.reshape(GROUPS, STORED, NX, NY, NZ)
    window = jax.vmap(pick_window)(grouped, band_ranking[:, :GB]).reshape(NB, NX, NY, NZ)
    states = jnp.take(pool_states, state_order[:NQ].astype(jnp.int32), axis=0).astype(jnp.float32)
    factor = 1.0 / math.sqrt(NX * NY * NZ)

    def transform(orbital):
        density = (orbital.astype(jnp.float32)[None] * states).astype(jnp.bfloat16)
        density = lax.optimization_barrier(density).astype(jnp.float32)
        spectrum = jnp.fft.fftn(density, axes=(1, 2, 3)).reshape(NQ, NX * NY * NZ)
        picked = jnp.take(spectrum, gvector_index.astype(jnp.int32), axis=1) * factor
        return jnp.stack([jnp.real(picked), jnp.imag(picked)], axis=1).astype(jnp.bfloat16)
    pair_fields = lax.optimization_barrier(lax.map(transform, window)).astype(jnp.float32)
    flat_pairs = pair_fields.reshape(NP * 2, NG)

    def block_sigma(first_row):
        tile_rows = lax.dynamic_slice_in_dim(screened, first_row, RB, 1).astype(jnp.float32).reshape(2 * RB, NG)
        products = jnp.dot(tile_rows, flat_pairs.T, precision=lax.Precision.HIGHEST, preferred_element_type=jnp.float32)
        products = products.reshape(2, RB, NB, NQ, 2)
        screened_real = products[0, :, :, :, 0] - products[1, :, :, :, 1]
        screened_imag = products[0, :, :, :, 1] + products[1, :, :, :, 0]
        left_pairs = lax.dynamic_slice_in_dim(pair_fields, first_row, RB, 3)
        highest = lax.Precision.HIGHEST
        real_part = jnp.einsum('mnr,rmk->nkm', left_pairs[:, :, 0], screened_real, precision=highest) + jnp.einsum('mnr,rmk->nkm', left_pairs[:, :, 1], screened_imag, precision=highest)
        imag_part = jnp.einsum('mnr,rmk->nkm', left_pairs[:, :, 0], screened_imag, precision=highest) - jnp.einsum('mnr,rmk->nkm', left_pairs[:, :, 1], screened_real, precision=highest)
        return jnp.stack([real_part, imag_part])
    starts = jnp.arange(NG // RB, dtype=jnp.int32) * RB
    return lax.optimization_barrier(jnp.sum(lax.map(block_sigma, starts), axis=0))
```

```python
import functools
import math

import jax
import jax.numpy as jnp
import numpy as np
from jax import lax
from jax.experimental import pallas as pl
from jax.experimental.pallas import tpu as pltpu
from jax.sharding import PartitionSpec as P

NX = 64
NY = 64
NZ = 128
GB = 16
NQ = 2
LANES = 128
SUBS = 8
COMPS = 4


def angles(length):
    indices = np.arange(length)
    return (indices[:, None] * indices[None, :] % length) * (2.0 * math.pi / length)


def real_table(length):
    turn = angles(length)
    return np.stack([np.cos(turn), -np.sin(turn)]).astype(np.float32)


def complex_table(length):
    turn = angles(length)
    cosine, sine = np.cos(turn), np.sin(turn)
    return np.stack([np.stack([cosine, -sine]), np.stack([sine, cosine])]).astype(np.float32)


def x_matrix(per_device):
    table = complex_table(NX).astype(np.float64) / math.sqrt(NX * NY * NZ)
    full = np.zeros((NX, COMPS, per_device, 2, NX), np.float64)
    for pair in range(per_device):
        for out in range(2):
            for part in range(2):
                full[:, 2 * pair + out, pair, part, :] = table[part, out].T
    return full.reshape(NX * COMPS, per_device * 2 * NX).astype(np.float32)


def split(value):
    high = value.astype(jnp.bfloat16)
    return high, (value - high.astype(jnp.float32)).astype(jnp.bfloat16)


def density_kernel(ranking_ref, order_ref, orbitals_ref, pool_ref, out_ref):
    def band(j, carry):
        orbital = orbitals_ref[ranking_ref[0, j]].astype(jnp.float32)
        for n in range(NQ):
            state = pool_ref[order_ref[n]].astype(jnp.float32)
            out_ref[j, n] = (orbital * state).astype(jnp.bfloat16)
        return carry

    lax.fori_loop(0, out_ref.shape[0], band, 0)


def densities(orbitals, band_ranking, pool_states, state_order):
    smem = pl.BlockSpec(memory_space=pltpu.SMEM)
    vmem = pl.BlockSpec(memory_space=pltpu.VMEM)
    return pl.pallas_call(
        density_kernel,
        out_shape=jax.ShapeDtypeStruct((GB, NQ) + orbitals.shape[1:], jnp.bfloat16),
        in_specs=[smem, smem, vmem, vmem],
        out_specs=vmem,
        compiler_params=pltpu.CompilerParams(vmem_limit_bytes=32 * 1024 * 1024),
    )(band_ranking, state_order, orbitals, pool_states)


def pick_kernel(row_ref, turn_ref, high_ref, low_ref, field_ref, out_ref, table, picked):
    def mm(a, b):
        return jnp.dot(a, b, preferred_element_type=jnp.float32)

    def transform(w, carry):
        data_high, data_low = split(field_ref[w])
        value = mm(high_ref[...], data_high) + (
            mm(high_ref[...], data_low) + mm(low_ref[...], data_high)
        )
        table[pl.ds(w * NX, NX)] = value.reshape(NX, COMPS, LANES)
        return carry

    lax.fori_loop(0, NY, transform, 0)
    lane = lax.broadcasted_iota(jnp.int32, (COMPS, LANES), 1)

    def block(b, carry):
        held = [jnp.zeros((COMPS, LANES), jnp.float32) for _ in range(4)]
        base = b * LANES
        for j in range(LANES):
            row = table[row_ref[base + j]]
            held[j % 4] = jnp.where(
                lane == j, pltpu.roll(row, turn_ref[base + j], 1), held[j % 4]
            )
        total = (held[0] + held[1]) + (held[2] + held[3])
        picked[b] = total
        return carry

    lax.fori_loop(0, picked.shape[0], block, 0)
    for c in range(out_ref.shape[0]):
        out_ref[c] = picked[:, c, :].astype(jnp.bfloat16)


def pick(field, gvector_index, per_device):
    count = gvector_index.shape[0]
    rows = (gvector_index // NZ) % NY * NX + gvector_index // (NY * NZ)
    turns = (jnp.arange(count, dtype=jnp.int32) - gvector_index % NZ) % LANES
    high, low = split(jnp.asarray(x_matrix(per_device)))
    smem = pl.BlockSpec(memory_space=pltpu.SMEM)
    vmem = pl.BlockSpec(memory_space=pltpu.VMEM)
    return pl.pallas_call(
        pick_kernel,
        out_shape=jax.ShapeDtypeStruct((2 * per_device, count // LANES, LANES), jnp.bfloat16),
        in_specs=[smem, smem, vmem, vmem, vmem],
        out_specs=vmem,
        scratch_shapes=[
            pltpu.VMEM((NX * NY, COMPS, LANES), jnp.float32),
            pltpu.VMEM((count // LANES, COMPS, LANES), jnp.float32),
        ],
        compiler_params=pltpu.CompilerParams(vmem_limit_bytes=56 * 1024 * 1024),
    )(rows, turns, high, low, field)


def swap_matrix(bands):
    full = np.zeros((SUBS, bands, bands, SUBS), np.float32)
    for s in range(SUBS):
        for m in range(bands):
            full[s, m, m, s] = 1.0
    return full.reshape(SUBS * bands, bands * SUBS)


def sigma_kernel(group, swap_ref, rows_ref, cols_ref, tile_ref, out_ref, left, right, total):
    step = pl.program_id(0)
    bands = rows_ref.shape[0]
    width = tile_ref.shape[2]

    @pl.when(step == 0)
    def _():
        total[...] = jnp.zeros_like(total)
        for source, target in ((rows_ref, left), (cols_ref, right)):
            for part in range(2):
                for n in range(NQ):
                    for m in range(0, bands, group):
                        first = (part * NQ + n) * bands + m

                        def move(s, carry):
                            rows = pl.ds(pl.multiple_of(s * SUBS, SUBS), SUBS)
                            data = source[m : m + group, n, part, rows, :].astype(jnp.float32)
                            data = data.reshape(group * SUBS, LANES).astype(jnp.bfloat16)
                            data = jnp.dot(
                                swap_ref[...], data, preferred_element_type=jnp.float32
                            ).astype(jnp.bfloat16)
                            for k in range(SUBS):
                                lanes = pl.ds(
                                    pl.multiple_of((s * SUBS + k) * LANES, LANES), LANES
                                )
                                target[first : first + group, lanes] = data[
                                    k * group : (k + 1) * group
                                ]
                            return carry

                        lax.fori_loop(0, source.shape[3] // SUBS, move, 0)

    depth = tile_ref.shape[1]
    half = NQ * bands
    a = jnp.dot(left[:, :depth], tile_ref[0], preferred_element_type=jnp.float32)
    b = jnp.dot(left[:, :depth], tile_ref[1], preferred_element_type=jnp.float32)
    real = a[:half] + b[half:]
    imag = b[:half] - a[half:]
    lanes = pl.ds(pl.multiple_of(step * width, width), width)
    other = right[:, lanes].astype(jnp.float32)
    for n in range(NQ):
        lr = real[n * bands : (n + 1) * bands]
        li = imag[n * bands : (n + 1) * bands]
        for k in range(NQ):
            qr = other[k * bands : (k + 1) * bands]
            qi = other[half + k * bands : half + (k + 1) * bands]
            re = lr * qr - li * qi
            im = lr * qi + li * qr
            for part, value in ((0, re), (1, im)):
                held = total[part, n, k]
                for piece in range(width // LANES):
                    held = held + value[:, piece * LANES : (piece + 1) * LANES]
                total[part, n, k] = held

    @pl.when(step == pl.num_programs(0) - 1)
    def _():
        out_ref[...] = total[...]


def sigma_tile(rows, cols, screened):
    bands = rows.shape[0]
    group = 32
    width = 512
    depth, columns = screened.shape[1:]
    extra = -rows.shape[3] % SUBS
    if extra:
        rows = jnp.pad(rows, ((0, 0),) * 3 + ((0, extra), (0, 0)))
    swap = jnp.asarray(swap_matrix(group)).astype(jnp.bfloat16)
    whole = pl.BlockSpec(memory_space=pltpu.VMEM)
    return pl.pallas_call(
        functools.partial(sigma_kernel, group),
        grid=(columns // width,),
        out_shape=jax.ShapeDtypeStruct((2, NQ, NQ, bands, LANES), jnp.float32),
        in_specs=[whole, whole, whole, pl.BlockSpec((2, depth, width), lambda i: (0, 0, i))],
        out_specs=pl.BlockSpec((2, NQ, NQ, bands, LANES), lambda i: (0, 0, 0, 0, 0)),
        scratch_shapes=[
            pltpu.VMEM((2 * NQ * bands, rows.shape[3] * LANES), jnp.bfloat16),
            pltpu.VMEM((2 * NQ * bands, columns), jnp.bfloat16),
            pltpu.VMEM((2, NQ, NQ, bands, LANES), jnp.float32),
        ],
        compiler_params=pltpu.CompilerParams(vmem_limit_bytes=56 * 1024 * 1024),
    )(swap, rows, cols, screened)


def body(orbitals, band_ranking, pool_states, state_order, gvector_index, screened):
    accurate = lax.Precision.HIGH
    x_local = orbitals.shape[1]
    y_local = orbitals.shape[2]
    row_devices = lax.axis_size("row")
    col_devices = lax.axis_size("col")
    band_devices = lax.axis_size("band")
    pair_count = GB * NQ
    per_device = pair_count // (row_devices * col_devices)
    density = densities(orbitals, band_ranking, pool_states, state_order)
    density = density.reshape(pair_count, x_local, y_local, NZ)
    received = lax.all_to_all(density, ("row", "col"), split_axis=0, concat_axis=0, tiled=True)
    received = received.reshape(row_devices, col_devices, per_device, x_local, y_local, NZ)
    y_table = jnp.asarray(complex_table(NY)).reshape(2, 2, col_devices, y_local, NY)
    z_table = jnp.asarray(real_table(NZ))
    field = jnp.einsum(
        "rcpxyz,bzk->bprcxyk", received.astype(jnp.float32), z_table, precision=accurate
    )
    field = jnp.einsum("aprcxyz,abcyw->wpbrxz", field, y_table, precision=accurate)
    field = field.reshape(NY, per_device * 2 * NX, NZ)
    own = pick(field, gvector_index, per_device)

    own = own.reshape(per_device, 2, -1, LANES)
    others = band_devices * row_devices
    by_col = own.reshape(per_device, 2, col_devices, -1, LANES)
    by_col = lax.all_to_all(by_col, "col", split_axis=2, concat_axis=0, tiled=False)
    cols = lax.all_gather(by_col, ("band", "row"), axis=0, tiled=False)
    by_row = own.reshape(per_device, 2, others, -1, LANES)
    by_row = lax.all_to_all(by_row, ("band", "row"), split_axis=2, concat_axis=0, tiled=False)
    rows = lax.all_gather(by_row, "col", axis=1, tiled=False)
    bands = band_devices * GB
    cols = cols.reshape(bands, NQ, 2, -1, LANES)
    rows = rows.reshape(bands, NQ, 2, -1, LANES)
    share = jnp.sum(sigma_tile(rows, cols, screened), axis=-1)
    shares = lax.all_gather(share, ("band", "row", "col"), axis=0, tiled=False)
    return jnp.sum(shares, axis=0)


def solution(mesh):
    placed = (
        P("band", "row", "col", None),
        P("band", None),
        P(None, "row", "col", None),
        P(),
        P(),
        P(None, ("band", "row"), "col"),
    )
    return jax.shard_map(body, mesh=mesh, in_specs=placed, out_specs=P(), check_vma=False)
```
